32 devices in a mesh: section: 4 (over x, core), ctx: 2 (over y), dp: 4 (over z).
Axes of the slice: x: 2, y: 2, z: 4, core: 2. Of those that a mesh axis runs over, the one named last changes fastest.
Arguments:
- inputs: bfloat16 [4, 512, 4096], P('section', 'ctx', 'dp'), may hold values from -6 to 6
- upstream: bfloat16 [4, 512, 4096], P('section', 'ctx', 'dp'), may hold values from -6 to 6
- short_filter: bfloat16 [4, 21, 256], P('section', None, 'dp'), may hold values from -2 to 2
- medium_filter: bfloat16 [4, 128, 256], P('section', None, 'dp'), may hold values from -0.5 to 0.5
Outputs:
- incoming: bfloat16 [4, 512, 4096], P('section', 'ctx', 'dp')
- grad_short: float32 [4, 21, 256], P('section', None, ('dp', 'ctx'))
- grad_medium: float32 [4, 128, 256], P('section', None, ('dp', 'ctx'))
The draws below stay inside these ranges and needn't reach their ends.
All inputs are finite; a program needn't handle non-finite values.
Results may differ from the reference program's by a relative error of at most 0.0071.
Values may be sent and summed in bfloat16 or wider, within the bound.
A program may use at most 64 MiB of HBM per device.

```python
import jax
import jax.numpy as jnp
from jax import lax

C = 4096
SK = 7
MK = 128
G = 256
SECTIONS = 4
SEQ = 512


def raised(drawn, stream_key, source, target, parts, factor):
    owner, partner = [(jnp.arange(drawn.shape[dim]) // (drawn.shape[dim] // parts)).reshape([-1 if axis == dim else 1 for axis in range(drawn.ndim)]) for dim in (source, target)]
    chosen = jax.random.permutation(stream_key, parts)[partner]
    strong = (owner == chosen) | (owner == (partner + parts // 2) % parts)
    return jnp.where(strong, factor * drawn, drawn)


def levels(key, shape, shards, low, largest):
    loudness, own = 1.0, jax.random.fold_in(key, 6)
    for position, blocks in shards:
        heights = jnp.exp(jax.random.uniform(jax.random.fold_in(own, position), (blocks,), jnp.float32, low / len(shards), largest / len(shards)))
        loudness = loudness * jnp.repeat(heights, shape[position] // blocks).reshape([-1 if axis == position else 1 for axis in range(len(shape))])
    return loudness


def gaussian(key, dims, scale, most, cuts=(), kind=jnp.bfloat16):
    entries = jax.random.normal(key, dims, jnp.float32) * scale
    if len(cuts) > 0:
        entries = levels(key, dims, cuts, -0.22, 0.18) * entries
    return jnp.clip(entries, min=-most, max=most).astype(kind)


def bell_draw_with(rng, dims, spread, most, split, heavy, kind=jnp.bfloat16):
    result = spread * jax.random.normal(rng, dims, jnp.float32)
    if split:
        result = result * levels(rng, dims, split, -0.22, 0.18)
    return jnp.clip(raised(result, jax.random.fold_in(rng, 3), *heavy), -most, most).astype(kind)


def setup_inputs(seed: int = 0) -> dict:
    keys = jax.random.split(jax.random.key(seed), 5)
    inputs = gaussian(keys[0], (SECTIONS, SEQ, C), 1.0, 6.0, ((0, 4), (1, 2), (2, 4)))
    upstream = bell_draw_with(keys[1], (SECTIONS, SEQ, C), 1.0, 6.0, ((0, 4), (1, 2), (2, 4)), (1, 2, 4, 2.0))
    short_filter = gaussian(keys[2], (SECTIONS, 3 * SK, G), SK ** -0.5, 2.0, ((0, 4), (2, 4)))
    medium_filter = gaussian(keys[3], (SECTIONS, MK, G), MK ** -0.5, 0.5, ((0, 4), (2, 4)))
    return dict(inputs=inputs, upstream=upstream, short_filter=short_filter, medium_filter=medium_filter)


def causal_mix(signal, taps):
    length = signal.shape[0] + taps.shape[0]
    spectrum = jnp.fft.rfft(signal, n=length, axis=0) * jnp.fft.rfft(taps, n=length, axis=0)
    return jnp.fft.irfft(spectrum, n=length, axis=0)[: signal.shape[0]].astype(signal.dtype)


def lagged(values_in, offset):
    return jnp.pad(values_in, ((offset, 0), (0, 0)))[: values_in.shape[0]]


def leading(values_in, offset):
    return jnp.pad(values_in, ((0, offset), (0, 0)))[offset:]


def one_section(operands):
    signal, grad_out, short_taps, medium_taps = operands
    seq_len, chan_count = signal.shape
    group_count = medium_taps.shape[1]
    group_width = chan_count // group_count
    chan_short = jnp.repeat(short_taps.astype(jnp.float32).reshape(3, SK, group_count), group_width, axis=2)
    chan_medium = jnp.repeat(medium_taps.astype(jnp.float32), group_width, axis=1)
    signal_f = signal.astype(jnp.float32)
    features = []
    for branch in range(3):
        running = jnp.zeros((seq_len, chan_count), jnp.float32)
        for offset in range(SK):
            running = running + chan_short[branch, offset] * lagged(signal_f, offset)
        features.append(running.astype(jnp.bfloat16))
    query_in, key_in, value_in = features
    products = (key_in.astype(jnp.float32) * value_in.astype(jnp.float32)).astype(jnp.bfloat16)
    mixed_out = causal_mix(products.astype(jnp.float32), chan_medium)
    grad_f = grad_out.astype(jnp.float32)
    query_grad = (grad_f * mixed_out).astype(jnp.bfloat16)
    gate_grad = (grad_f * query_in.astype(jnp.float32)).astype(jnp.bfloat16)
    kv_grad = jnp.flip(causal_mix(jnp.flip(gate_grad.astype(jnp.float32), 0), chan_medium), 0)
    key_grad = (kv_grad * value_in.astype(jnp.float32)).astype(jnp.bfloat16)
    value_grad = (kv_grad * key_in.astype(jnp.float32)).astype(jnp.bfloat16)
    input_grad = jnp.zeros((seq_len, chan_count), jnp.float32)
    short_rows = []
    for branch, feature_grad in enumerate([query_grad, key_grad, value_grad]):
        feature_f = feature_grad.astype(jnp.float32)
        for offset in range(SK):
            input_grad = input_grad + chan_short[branch, offset] * leading(feature_f, offset)
            short_rows.append(jnp.sum(feature_f * lagged(signal_f, offset), axis=0))
    short_grad = jnp.stack(short_rows).reshape(3 * SK, group_count, group_width).sum(-1)
    length = seq_len + MK
    spectrum = jnp.fft.rfft(gate_grad.astype(jnp.float32), n=length, axis=0) * jnp.conj(jnp.fft.rfft(products.astype(jnp.float32), n=length, axis=0))
    medium_grad = jnp.fft.irfft(spectrum, n=length, axis=0)[:MK].astype(signal_f.dtype)
    medium_grad = medium_grad.reshape(MK, group_count, group_width).sum(-1)
    return input_grad.astype(jnp.bfloat16), short_grad, medium_grad


def reference(inputs, upstream, short_filter, medium_filter):
    input_grad, short_grad, medium_grad = lax.map(one_section, (inputs, upstream, short_filter, medium_filter))
    incoming = jnp.concatenate([input_grad[1:], jnp.zeros_like(input_grad[:1])], 0)
    return incoming, short_grad, medium_grad
```

```python
from functools import partial

import jax
import jax.numpy as jnp
from jax import lax
from jax.experimental import pallas as pl
from jax.experimental.pallas import tpu as pltpu
from jax.sharding import PartitionSpec as P

MESH = pl.DeviceIdType.MESH
F32 = jnp.float32
BF16 = jnp.bfloat16
LANES = 128
RIM = 8
CHUNK = 64


def iota(shape, dim):
    return lax.broadcasted_iota(jnp.int32, shape, dim)


def kernel(
    dims,
    x_ref, gy_ref, sf_ref, mf_ref,
    out_ref, gs_ref, gm_ref,
    hf, hb, wsc, tm, tk, xf, xrim, kvp, gext, keyb, valb, ef, ot, zb, grads, snd, rcv, tr,
    bx_s, bx_r, kv_s, kv_r, ga_s, ga_r, er_s, er_r, ou_s, ou_r, gr_s, gr_r, z_sem,
):
    n_ctx, n_sec, rows, tiles, lags, taps, width = dims
    c = lax.axis_index("ctx")
    s = lax.axis_index("section")
    nxt = lax.rem(c + 1, n_ctx)
    prv = lax.rem(c + n_ctx - 1, n_ctx)
    has_next = c < n_ctx - 1
    has_prev = c > 0
    sends_out = s > 0
    gets_out = s < n_sec - 1
    down = lax.rem(s + n_sec - 1, n_sec)
    up = lax.rem(s + 1, n_sec)
    gpt = LANES // width
    groups = gpt * tiles
    gpd = groups // n_ctx
    nb = rows // taps
    span = 2 * taps
    features = 3

    barrier = pltpu.get_barrier_semaphore()
    for d in range(1, n_ctx):
        pl.semaphore_signal(
            barrier, inc=1, device_id={"ctx": lax.rem(c + d, n_ctx)}, device_id_type=MESH
        )

    @pl.when(sends_out)
    def _():
        pl.semaphore_signal(barrier, inc=1, device_id={"section": down}, device_id_type=MESH)

    @pl.when(gets_out)
    def _():
        pl.semaphore_signal(barrier, inc=1, device_id={"section": up}, device_id_type=MESH)

    def remote(src, dst, send, recv, where):
        return pltpu.make_async_remote_copy(
            src_ref=src, dst_ref=dst, send_sem=send, recv_sem=recv,
            device_id=where, device_id_type=MESH,
        )

    def x_copy():
        return remote(
            x_ref.at[0, pl.ds(rows - 16, 16)], xrim, bx_s.at[0], bx_r.at[0], {"ctx": nxt}
        )

    def kv_copy(k):
        return remote(
            kvp.at[k, pl.ds(rows, taps)], kvp.at[k, pl.ds(0, taps)],
            kv_s.at[k], kv_r.at[k], {"ctx": nxt},
        )

    def gate_copy(k):
        return remote(
            gext.at[k, pl.ds(0, taps)], gext.at[k, pl.ds(rows, taps)],
            ga_s.at[k], ga_r.at[k], {"ctx": prv},
        )

    def rim_copy(k):
        return remote(
            ef.at[k, :, pl.ds(0, RIM)], ef.at[k, :, pl.ds(rows, RIM)],
            er_s.at[k], er_r.at[k], {"ctx": prv},
        )

    def out_copy(k):
        return remote(
            ot.at[k], out_ref.at[0, :, pl.ds(pl.multiple_of(k * LANES, LANES), LANES)],
            ou_s.at[k], ou_r.at[k], {"section": down},
        )

    taps_in = mf_ref[0]
    dot_tn = partial(
        lax.dot_general, dimension_numbers=(((0,), (0,)), ((), ())), preferred_element_type=F32
    )
    dot_nt = partial(
        lax.dot_general, dimension_numbers=(((1,), (1,)), ((), ())), preferred_element_type=F32
    )
    row_j, col_m = iota((taps, span), 0), iota((taps, span), 1)
    flipped = dot_tn(taps_in, (col_m == taps - row_j).astype(BF16))
    straight = dot_tn(taps_in, (col_m == row_j).astype(BF16))
    spread = (iota((groups, tiles * LANES), 1) // width == iota((groups, tiles * LANES), 0))
    wide = jnp.dot(sf_ref[0], spread.astype(BF16), preferred_element_type=F32)
    for k in range(tiles):
        hf[k] = flipped[k * gpt : (k + 1) * gpt]
        hb[k] = straight[k * gpt : (k + 1) * gpt]
        wsc[k, 0 : features * lags] = wide[:, k * LANES : (k + 1) * LANES]

    def build(k, carry):
        for u in range(gpt):
            for rows_of, dest in ((hf, tm), (hb, tk)):
                line = jnp.broadcast_to(rows_of[k, u : u + 1], (taps, span))
                band = pltpu.roll(line, 0, 1, stride=1, stride_axis=0)
                dest[k, :, u * span : (u + 1) * span] = band.astype(BF16)
        return carry

    lax.fori_loop(0, tiles // 2, build, 0)

    pl.semaphore_wait(
        barrier, n_ctx - 1 + sends_out.astype(jnp.int32) + gets_out.astype(jnp.int32)
    )

    @pl.when(has_next)
    def _():
        x_copy().start()

    @pl.when(jnp.logical_not(has_prev))
    def _():
        xrim[...] = jnp.zeros_like(xrim)
        kvp[:, 0:taps] = jnp.zeros((tiles, taps, LANES), BF16)

    @pl.when(jnp.logical_not(has_next))
    def _():
        gext[:, rows : rows + taps] = jnp.zeros((tiles, taps, LANES), BF16)
        ef[:, :, rows : rows + RIM] = jnp.zeros((tiles, features, RIM, LANES), F32)

    def zero_copy():
        return pltpu.make_async_copy(zb, out_ref.at[0], z_sem.at[0])

    @pl.when(jnp.logical_not(gets_out))
    def _():
        zb[...] = jnp.zeros_like(zb)
        zero_copy().start()

    lax.fori_loop(tiles // 2, tiles, build, 0)

    @pl.when(has_prev)
    def _():
        x_copy().wait_recv()

    def lane_slice(k):
        return pl.ds(pl.multiple_of(k * LANES, LANES), LANES)

    def feature_tile(k, carry):
        xf[k, RIM : RIM + rows] = x_ref[0, :, lane_slice(k)].astype(F32)
        xf[k, 0:RIM] = xrim[:, lane_slice(k)].astype(F32)[16 - RIM :]
        for start in range(0, rows, CHUNK):
            sums = [jnp.zeros((CHUNK, LANES), F32) for _ in range(features)]
            for i in range(lags):
                window = xf[k, RIM + start - i : RIM + start - i + CHUNK]
                for f in range(features):
                    sums[f] = sums[f] + wsc[k, f * lags + i : f * lags + i + 1] * window
            q, key, val = [v.astype(BF16) for v in sums]
            here = slice(start, start + CHUNK)
            keyb[k, here] = key
            valb[k, here] = val
            kvp[k, taps + start : taps + start + CHUNK] = (
                key.astype(F32) * val.astype(F32)
            ).astype(BF16)
            gext[k, here] = (
                gy_ref[0, here, lane_slice(k)].astype(F32) * q.astype(F32)
            ).astype(BF16)

        @pl.when(has_next)
        def _():
            kv_copy(k).start()

        @pl.when(has_prev)
        def _():
            gate_copy(k).start()

        return carry

    lax.fori_loop(0, tiles, feature_tile, 0)

    lane_group = lax.rem(iota((1, nb * LANES), 1), LANES) // width
    masks = [(lane_group == u).astype(BF16) for u in range(gpt)]
    reverse = (iota((taps, taps), 0) + iota((taps, taps), 1) == taps - 1).astype(BF16)

    def windows(ref, k):
        return jnp.concatenate(
            [ref[k, b * taps : b * taps + span] for b in range(nb)], axis=1
        )

    def medium_tile(k):
        @pl.when(has_prev)
        def _():
            kv_copy(k).wait_recv()

        @pl.when(has_next)
        def _():
            gate_copy(k).wait_recv()

        kv_win = windows(kvp, k)
        gate_win = windows(gext, k)
        mixed = jnp.zeros((taps, nb * LANES), F32)
        back = jnp.zeros((taps, nb * LANES), F32)
        for u in range(gpt):
            cols = slice(u * span, (u + 1) * span)
            mixed = mixed + jnp.dot(
                tm[k, :, cols], kv_win * masks[u], preferred_element_type=F32
            )
            back = back + jnp.dot(
                tk[k, :, cols], gate_win * masks[u], preferred_element_type=F32
            )
        for b in range(nb):
            here = slice(b * taps, (b + 1) * taps)
            mix_b = mixed[:, b * LANES : (b + 1) * LANES]
            back_b = back[:, b * LANES : (b + 1) * LANES]
            ef[k, 0, here] = (
                gy_ref[0, here, lane_slice(k)].astype(F32) * mix_b
            ).astype(BF16).astype(F32)
            ef[k, 1, here] = (back_b * valb[k, here].astype(F32)).astype(BF16).astype(F32)
            ef[k, 2, here] = (back_b * keyb[k, here].astype(F32)).astype(BF16).astype(F32)

        @pl.when(has_prev)
        def _():
            rim_copy(k).start()

        kv_own = jnp.concatenate(
            [kvp[k, taps + b * taps : span + b * taps] for b in range(nb)], axis=1
        )
        kv_rev = jnp.dot(reverse, kv_own, preferred_element_type=F32).astype(BF16)
        lines = []
        for u in range(gpt):
            cross = dot_nt(kv_rev * masks[u], gate_win)
            turned = pltpu.roll(cross, 0, 1, stride=1, stride_axis=0)
            lines.append(jnp.sum(turned, axis=0, keepdims=True))
        diag = pltpu.roll(jnp.concatenate(lines, axis=0), span - taps + 1, 1)
        grads[pl.ds(pl.multiple_of(k * gpt, gpt), gpt), 0:taps] = diag[:, 0:taps]

    gather = (iota((gpt, LANES), 1) // width == iota((gpt, LANES), 0)).astype(F32)

    def short_tile(k):
        @pl.when(has_next)
        def _():
            rim_copy(k).wait_recv()

        sums = [jnp.zeros((8, LANES), F32) for _ in range(features * lags)]
        for start in range(0, rows, CHUNK):
            x_here = xf[k, RIM + start : RIM + start + CHUNK]
            total = jnp.zeros((CHUNK, LANES), F32)
            for f in range(features):
                for i in range(lags):
                    at = f * lags + i
                    e = ef[k, f, start + i : start + i + CHUNK]
                    total = total + wsc[k, at : at + 1] * e
                    sums[at] = sums[at] + jnp.sum(
                        (e * x_here).reshape(CHUNK // 8, 8, LANES), axis=0
                    )
            ot[k, start : start + CHUNK] = total.astype(BF16)

        @pl.when(sends_out)
        def _():
            out_copy(k).start()

        flat = [jnp.sum(v, axis=0, keepdims=True) for v in sums]
        flat.append(jnp.zeros((LANES - features * lags, LANES), F32))
        flat = jnp.concatenate(flat, axis=0)
        grads[pl.ds(pl.multiple_of(k * gpt, gpt), gpt), taps : taps + LANES] = dot_nt(
            gather, flat, precision=lax.Precision.HIGHEST
        )

    lag = 2

    def step(k, carry):
        @pl.when(k < tiles)
        def _():
            medium_tile(k)

        @pl.when(k >= lag)
        def _():
            short_tile(k - lag)

        return carry

    lax.fori_loop(0, tiles + lag, step, 0)

    for p in range(n_ctx):
        snd[p] = grads[p * gpd : (p + 1) * gpd]

    def grad_copy(d):
        to = lax.rem(c + d, n_ctx)
        return remote(snd.at[to], rcv.at[d - 1], gr_s.at[d - 1], gr_r.at[d - 1], {"ctx": to})

    for d in range(1, n_ctx):
        grad_copy(d).start()
    total = snd[c]
    for d in range(1, n_ctx):
        grad_copy(d).wait_recv()
        total = total + rcv[d - 1]
    tr[...] = jnp.zeros_like(tr)
    tr[0:gpd] = total
    gm_ref[0] = tr[:, 0:taps].T[:, 0:gpd]
    gs_ref[0] = tr[:, taps : taps + LANES].T[0 : features * lags, 0:gpd]

    for d in range(1, n_ctx):
        grad_copy(d).wait_send()

    @pl.when(has_next)
    def _():
        x_copy().wait_send()

    def drain(k, carry):
        @pl.when(has_next)
        def _():
            kv_copy(k).wait_send()

        @pl.when(has_prev)
        def _():
            gate_copy(k).wait_send()
            rim_copy(k).wait_send()

        @pl.when(sends_out)
        def _():
            out_copy(k).wait_send()

        @pl.when(gets_out)
        def _():
            out_copy(k).wait_recv()

        return carry

    lax.fori_loop(0, tiles, drain, 0)

    @pl.when(jnp.logical_not(gets_out))
    def _():
        zero_copy().wait()


def per_device(n_ctx, n_sec, inputs, upstream, short_filter, medium_filter):
    _, rows, chans = inputs.shape
    taps, groups = medium_filter.shape[1:]
    lags = short_filter.shape[1] // 3
    width = chans // groups
    tiles = chans // LANES
    gpt = LANES // width
    gpd = groups // n_ctx
    dims = (n_ctx, n_sec, rows, tiles, lags, taps, width)
    vmem = pl.BlockSpec(memory_space=pltpu.VMEM)
    dma = pltpu.SemaphoreType.DMA
    span = 2 * taps
    return pl.pallas_call(
        partial(kernel, dims),
        out_shape=(
            jax.ShapeDtypeStruct(inputs.shape, BF16),
            jax.ShapeDtypeStruct((1, 3 * lags, gpd), F32),
            jax.ShapeDtypeStruct((1, taps, gpd), F32),
        ),
        in_specs=[vmem] * 4,
        out_specs=(pl.BlockSpec(memory_space=pl.ANY), vmem, vmem),
        scratch_shapes=[
            pltpu.VMEM((tiles, gpt, span), F32),
            pltpu.VMEM((tiles, gpt, span), F32),
            pltpu.VMEM((tiles, 24, LANES), F32),
            pltpu.VMEM((tiles, taps, gpt * span), BF16),
            pltpu.VMEM((tiles, taps, gpt * span), BF16),
            pltpu.VMEM((tiles, rows + RIM, LANES), F32),
            pltpu.VMEM((16, chans), BF16),
            pltpu.VMEM((tiles, rows + taps, LANES), BF16),
            pltpu.VMEM((tiles, rows + taps, LANES), BF16),
            pltpu.VMEM((tiles, rows, LANES), BF16),
            pltpu.VMEM((tiles, rows, LANES), BF16),
            pltpu.VMEM((tiles, 3, rows + RIM, LANES), F32),
            pltpu.VMEM((tiles, rows, LANES), BF16),
            pltpu.VMEM((rows, chans), BF16),
            pltpu.VMEM((groups, taps + LANES), F32),
            pltpu.VMEM((n_ctx, gpd, taps + LANES), F32),
            pltpu.VMEM((max(n_ctx - 1, 1), gpd, taps + LANES), F32),
            pltpu.VMEM((LANES, taps + LANES), F32),
            dma((1,)), dma((1,)),
            dma((tiles,)), dma((tiles,)),
            dma((tiles,)), dma((tiles,)),
            dma((tiles,)), dma((tiles,)),
            dma((tiles,)), dma((tiles,)),
            dma((max(n_ctx - 1, 1),)), dma((max(n_ctx - 1, 1),)),
            dma((1,)),
        ],
        compiler_params=pltpu.CompilerParams(
            collective_id=0, has_side_effects=True, vmem_limit_bytes=40 * 1024 * 1024
        ),
    )(inputs, upstream, short_filter, medium_filter)


def solution(mesh):
    in_specs = (
        P("section", "ctx", "dp"),
        P("section", "ctx", "dp"),
        P("section", None, "dp"),
        P("section", None, "dp"),
    )
    out_specs = (
        P("section", "ctx", "dp"),
        P("section", None, ("dp", "ctx")),
        P("section", None, ("dp", "ctx")),
    )
    return jax.shard_map(
        partial(per_device, mesh.shape["ctx"], mesh.shape["section"]),
        mesh=mesh, in_specs=in_specs, out_specs=out_specs, check_vma=False,
    )
```

```python
from functools import partial

import jax
import jax.numpy as jnp
from jax import lax
from jax.experimental import pallas as pl
from jax.experimental.pallas import tpu as pltpu
from jax.sharding import PartitionSpec as P

MESH = pl.DeviceIdType.MESH
F32 = jnp.float32
BF16 = jnp.bfloat16
LANES = 128
RIM = 8
CHUNK = 64


def iota(shape, dim):
    return lax.broadcasted_iota(jnp.int32, shape, dim)


def kernel(
    dims,
    x_ref, gy_ref, sf_ref, mf_ref,
    out_ref, gs_ref, gm_ref,
    xv, gyv, hf, hb, wsc, tm, tk, xf, xrim, kvp, gext, keyb, valb, ef, ot, zb, grads_m, grads_s, snd, rcv, tr,
    bx_s, bx_r, kv_s, kv_r, ga_s, ga_r, er_s, er_r, ou_s, ou_r, gr_s, gr_r, z_sem, in_sem,
):
    n_ctx, n_sec, rows, tiles, lags, taps, width = dims
    c = lax.axis_index("ctx")
    s = lax.axis_index("section")
    nxt = lax.rem(c + 1, n_ctx)
    prv = lax.rem(c + n_ctx - 1, n_ctx)
    has_next = c < n_ctx - 1
    has_prev = c > 0
    sends_out = s > 0
    gets_out = s < n_sec - 1
    down = lax.rem(s + n_sec - 1, n_sec)
    up = lax.rem(s + 1, n_sec)
    gpt = LANES // width
    groups = gpt * tiles
    gpd = groups // n_ctx
    nb = rows // taps
    span = 2 * taps
    features = 3

    def load_x():
        return pltpu.make_async_copy(x_ref.at[0], xv, in_sem.at[0])

    def load_gy():
        return pltpu.make_async_copy(gy_ref.at[0], gyv, in_sem.at[1])

    load_x().start()
    load_gy().start()

    barrier = pltpu.get_barrier_semaphore()
    for d in range(1, n_ctx):
        pl.semaphore_signal(
            barrier, inc=1, device_id={"ctx": lax.rem(c + d, n_ctx)}, device_id_type=MESH
        )

    @pl.when(sends_out)
    def _():
        pl.semaphore_signal(barrier, inc=1, device_id={"section": down}, device_id_type=MESH)

    @pl.when(gets_out)
    def _():
        pl.semaphore_signal(barrier, inc=1, device_id={"section": up}, device_id_type=MESH)

    def remote(src, dst, send, recv, where):
        return pltpu.make_async_remote_copy(
            src_ref=src, dst_ref=dst, send_sem=send, recv_sem=recv,
            device_id=where, device_id_type=MESH,
        )

    def x_copy():
        return remote(
            x_ref.at[0, pl.ds(rows - 16, 16)], xrim, bx_s.at[0], bx_r.at[0], {"ctx": nxt}
        )

    def kv_copy(k):
        return remote(
            kvp.at[k, pl.ds(rows, taps)], kvp.at[k, pl.ds(0, taps)],
            kv_s.at[k], kv_r.at[k], {"ctx": nxt},
        )

    def gate_copy(k):
        return remote(
            gext.at[k, pl.ds(0, taps)], gext.at[k, pl.ds(rows, taps)],
            ga_s.at[k], ga_r.at[k], {"ctx": prv},
        )

    def rim_copy(k):
        return remote(
            ef.at[k, :, pl.ds(0, RIM)], ef.at[k, :, pl.ds(rows, RIM)],
            er_s.at[k], er_r.at[k], {"ctx": prv},
        )

    def out_copy(k):
        return remote(
            ot.at[k], out_ref.at[k],
            ou_s.at[k], ou_r.at[k], {"section": down},
        )

    taps_in = mf_ref[0]
    dot_nt = partial(
        lax.dot_general, dimension_numbers=(((1,), (1,)), ((), ())), preferred_element_type=F32
    )
    row_j, col_m = iota((taps, span), 0), iota((taps, span), 1)
    flipped = jnp.dot(
        taps_in, (col_m == taps - row_j).astype(BF16), preferred_element_type=F32
    )
    straight = jnp.dot(taps_in, (col_m == row_j).astype(BF16), preferred_element_type=F32)
    spread = (iota((groups, tiles * LANES), 1) // width == iota((groups, tiles * LANES), 0))
    wide = jnp.dot(sf_ref[0], spread.astype(BF16), preferred_element_type=F32)
    for k in range(tiles):
        hf[k] = flipped[k * gpt : (k + 1) * gpt]
        hb[k] = straight[k * gpt : (k + 1) * gpt]
        wsc[k, 0 : features * lags] = wide[:, k * LANES : (k + 1) * LANES]

    def build(k, carry):
        for u in range(gpt):
            for rows_of, dest in ((hf, tm), (hb, tk)):
                line = jnp.broadcast_to(rows_of[k, u : u + 1], (taps, span))
                band = pltpu.roll(line, 0, 1, stride=1, stride_axis=0)
                dest[k, :, u * span : (u + 1) * span] = band.astype(BF16)
        return carry

    lax.fori_loop(0, tiles // 2, build, 0)

    pl.semaphore_wait(
        barrier, n_ctx - 1 + sends_out.astype(jnp.int32) + gets_out.astype(jnp.int32)
    )

    @pl.when(has_next)
    def _():
        x_copy().start()

    @pl.when(jnp.logical_not(has_prev))
    def _():
        xrim[...] = jnp.zeros_like(xrim)
        kvp[:, 0:taps] = jnp.zeros((tiles, taps, LANES), BF16)

    @pl.when(jnp.logical_not(has_next))
    def _():
        gext[:, rows : rows + taps] = jnp.zeros((tiles, taps, LANES), BF16)
        ef[:, :, rows : rows + RIM] = jnp.zeros((tiles, features, RIM, LANES), F32)

    def zero_copy():
        return pltpu.make_async_copy(zb, out_ref, z_sem.at[0])

    @pl.when(jnp.logical_not(gets_out))
    def _():
        zb[...] = jnp.zeros_like(zb)
        zero_copy().start()

    lax.fori_loop(tiles // 2, tiles, build, 0)

    @pl.when(has_prev)
    def _():
        x_copy().wait_recv()

    load_x().wait()
    load_gy().wait()

    def lane_slice(k):
        return pl.ds(pl.multiple_of(k * LANES, LANES), LANES)

    def feature_tile(k, carry):
        xf[k, RIM : RIM + rows] = xv[:, lane_slice(k)].astype(F32)
        xf[k, 0:RIM] = xrim[:, lane_slice(k)].astype(F32)[16 - RIM :]
        for start in range(0, rows, CHUNK):
            sums = [jnp.zeros((CHUNK, LANES), F32) for _ in range(features)]
            for i in range(lags):
                window = xf[k, RIM + start - i : RIM + start - i + CHUNK]
                for f in range(features):
                    sums[f] = sums[f] + wsc[k, f * lags + i : f * lags + i + 1] * window
            q, key, val = [v.astype(BF16) for v in sums]
            here = slice(start, start + CHUNK)
            keyb[k, here] = key
            valb[k, here] = val
            kvp[k, taps + start : taps + start + CHUNK] = (
                key.astype(F32) * val.astype(F32)
            ).astype(BF16)
            gext[k, here] = (
                gyv[here, lane_slice(k)].astype(F32) * q.astype(F32)
            ).astype(BF16)

        @pl.when(has_next)
        def _():
            kv_copy(k).start()

        @pl.when(has_prev)
        def _():
            gate_copy(k).start()

        return carry

    lax.fori_loop(0, tiles, feature_tile, 0)

    lane_group = lax.rem(iota((1, nb * LANES), 1), LANES) // width
    masks = [(lane_group == u).astype(BF16) for u in range(gpt)]
    reverse = (iota((taps, taps), 0) + iota((taps, taps), 1) == taps - 1).astype(BF16)

    def windows(ref, k):
        return jnp.concatenate(
            [ref[k, b * taps : b * taps + span] for b in range(nb)], axis=1
        )

    def medium_ready(k):
        @pl.when(has_prev)
        def _():
            kv_copy(k).wait_recv()

        @pl.when(has_next)
        def _():
            gate_copy(k).wait_recv()

    def medium_sent(k):
        @pl.when(has_prev)
        def _():
            rim_copy(k).start()

    def medium_tile(k):
        kv_win = windows(kvp, k)
        gate_win = windows(gext, k)
        kv_all = jnp.concatenate([kv_win * m for m in masks], axis=0)
        mixed = jnp.dot(tm[k], kv_all, preferred_element_type=F32)
        gate_all = jnp.concatenate([gate_win * m for m in masks], axis=0)
        back = jnp.dot(tk[k], gate_all, preferred_element_type=F32)
        for b in range(nb):
            here = slice(b * taps, (b + 1) * taps)
            mix_b = mixed[:, b * LANES : (b + 1) * LANES]
            back_b = back[:, b * LANES : (b + 1) * LANES]
            ef[k, 0, here] = (
                gyv[here, lane_slice(k)].astype(F32) * mix_b
            ).astype(BF16).astype(F32)
            ef[k, 1, here] = (back_b * valb[k, here].astype(F32)).astype(BF16).astype(F32)
            ef[k, 2, here] = (back_b * keyb[k, here].astype(F32)).astype(BF16).astype(F32)

        kv_own = jnp.concatenate(
            [kvp[k, taps + b * taps : span + b * taps] for b in range(nb)], axis=1
        )
        kv_rev = jnp.dot(reverse, kv_own, preferred_element_type=F32).astype(BF16)
        lines = []
        crosses = dot_nt(jnp.concatenate([kv_rev * m for m in masks], axis=0), gate_win)
        for u in range(gpt):
            cross = crosses[u * taps : (u + 1) * taps]
            turned = pltpu.roll(cross, 0, 1, stride=1, stride_axis=0)
            lines.append(jnp.sum(turned, axis=0, keepdims=True))
        diag = pltpu.roll(jnp.concatenate(lines, axis=0), span - taps + 1, 1)
        grads_m[pl.ds(pl.multiple_of(k * gpt, gpt), gpt), :] = diag[:, 0:taps]

    gather = (iota((gpt, LANES), 1) // width == iota((gpt, LANES), 0)).astype(F32)

    def short_ready(k):
        @pl.when(has_next)
        def _():
            rim_copy(k).wait_recv()

    def short_sent(k):
        @pl.when(sends_out)
        def _():
            out_copy(k).start()

    def short_tile(k):
        sums = [jnp.zeros((8, LANES), F32) for _ in range(features * lags)]
        for start in range(0, rows, CHUNK):
            x_here = xf[k, RIM + start : RIM + start + CHUNK]
            total = jnp.zeros((CHUNK, LANES), F32)
            for f in range(features):
                for i in range(lags):
                    at = f * lags + i
                    e = ef[k, f, start + i : start + i + CHUNK]
                    total = total + wsc[k, at : at + 1] * e
                    sums[at] = sums[at] + jnp.sum(
                        (e * x_here).reshape(CHUNK // 8, 8, LANES), axis=0
                    )
            ot[k, start : start + CHUNK] = total.astype(BF16)

        flat = [jnp.sum(v, axis=0, keepdims=True) for v in sums]
        flat.append(jnp.zeros((LANES - features * lags, LANES), F32))
        flat = jnp.concatenate(flat, axis=0)
        grads_s[pl.ds(pl.multiple_of(k * gpt, gpt), gpt), :] = dot_nt(
            gather, flat, precision=lax.Precision.HIGHEST
        )

    lag = 2
    for k in range(lag):
        medium_ready(k)
        medium_tile(k)
        medium_sent(k)

    def step(k, carry):
        medium_ready(k)
        short_ready(k - lag)
        short_tile(k - lag)
        medium_tile(k)
        medium_sent(k)
        short_sent(k - lag)
        return carry

    lax.fori_loop(lag, tiles, step, 0)
    for k in range(tiles - lag, tiles):
        short_ready(k)
        short_tile(k)
        short_sent(k)

    for p in range(n_ctx):
        snd[p, :, 0:taps] = grads_m[p * gpd : (p + 1) * gpd]
        snd[p, :, taps : taps + LANES] = grads_s[p * gpd : (p + 1) * gpd]

    def grad_copy(d):
        to = lax.rem(c + d, n_ctx)
        return remote(snd.at[to], rcv.at[d - 1], gr_s.at[d - 1], gr_r.at[d - 1], {"ctx": to})

    for d in range(1, n_ctx):
        grad_copy(d).start()
    total = snd[c]
    for d in range(1, n_ctx):
        grad_copy(d).wait_recv()
        total = total + rcv[d - 1]
    gm_ref[0] = total[:, 0:taps]
    tr[...] = jnp.zeros_like(tr)
    tr[0:gpd] = total[:, taps : taps + LANES]
    gs_ref[:, 0] = tr[...].T[0 : features * lags, 0:gpd]

    for d in range(1, n_ctx):
        grad_copy(d).wait_send()

    @pl.when(has_next)
    def _():
        x_copy().wait_send()

    def drain(k, carry):
        @pl.when(has_next)
        def _():
            kv_copy(k).wait_send()

        @pl.when(has_prev)
        def _():
            gate_copy(k).wait_send()
            rim_copy(k).wait_send()

        @pl.when(sends_out)
        def _():
            out_copy(k).wait_send()

        @pl.when(gets_out)
        def _():
            out_copy(k).wait_recv()

        return carry

    lax.fori_loop(0, tiles, drain, 0)

    @pl.when(jnp.logical_not(gets_out))
    def _():
        zero_copy().wait()


def place(tiles, tiled_ref, gs_in, gm_in, out_ref, gs_ref, gm_ref, sem):
    copies = [
        pltpu.make_async_copy(
            tiled_ref.at[k], out_ref.at[0, :, pl.ds(k * LANES, LANES)], sem.at[k]
        )
        for k in range(tiles)
    ]
    copies.append(pltpu.make_async_copy(gs_in, gs_ref, sem.at[tiles]))
    copies.append(pltpu.make_async_copy(gm_in, gm_ref, sem.at[tiles + 1]))
    for copy in copies:
        copy.start()
    for copy in copies:
        copy.wait()


def per_device(n_ctx, n_sec, inputs, upstream, short_filter, medium_filter):
    _, rows, chans = inputs.shape
    taps, groups = medium_filter.shape[1:]
    lags = short_filter.shape[1] // 3
    width = chans // groups
    tiles = chans // LANES
    gpt = LANES // width
    gpd = groups // n_ctx
    dims = (n_ctx, n_sec, rows, tiles, lags, taps, width)
    vmem = pl.BlockSpec(memory_space=pltpu.VMEM)
    dma = pltpu.SemaphoreType.DMA
    span = 2 * taps
    hbm = pl.BlockSpec(memory_space=pltpu.HBM)
    incoming, short_part, medium_part = pl.pallas_call(
        partial(kernel, dims),
        out_shape=(
            jax.ShapeDtypeStruct((tiles, rows, LANES), BF16),
            jax.ShapeDtypeStruct((3 * lags, 1, gpd), F32),
            jax.ShapeDtypeStruct((1, gpd, taps), F32),
        ),
        in_specs=[hbm, hbm, vmem, vmem],
        out_specs=(pl.BlockSpec(memory_space=pl.ANY), vmem, vmem),
        scratch_shapes=[
            pltpu.VMEM((rows, chans), BF16),
            pltpu.VMEM((rows, chans), BF16),
            pltpu.VMEM((tiles, gpt, span), F32),
            pltpu.VMEM((tiles, gpt, span), F32),
            pltpu.VMEM((tiles, 24, LANES), F32),
            pltpu.VMEM((tiles, taps, gpt * span), BF16),
            pltpu.VMEM((tiles, taps, gpt * span), BF16),
            pltpu.VMEM((tiles, rows + RIM, LANES), F32),
            pltpu.VMEM((16, chans), BF16),
            pltpu.VMEM((tiles, rows + taps, LANES), BF16),
            pltpu.VMEM((tiles, rows + taps, LANES), BF16),
            pltpu.VMEM((tiles, rows, LANES), BF16),
            pltpu.VMEM((tiles, rows, LANES), BF16),
            pltpu.VMEM((tiles, 3, rows + RIM, LANES), F32),
            pltpu.VMEM((tiles, rows, LANES), BF16),
            pltpu.VMEM((tiles, rows, LANES), BF16),
            pltpu.VMEM((groups, taps), F32),
            pltpu.VMEM((groups, LANES), F32),
            pltpu.VMEM((n_ctx, gpd, taps + LANES), F32),
            pltpu.VMEM((max(n_ctx - 1, 1), gpd, taps + LANES), F32),
            pltpu.VMEM((LANES, LANES), F32),
            dma((1,)), dma((1,)),
            dma((tiles,)), dma((tiles,)),
            dma((tiles,)), dma((tiles,)),
            dma((tiles,)), dma((tiles,)),
            dma((tiles,)), dma((tiles,)),
            dma((max(n_ctx - 1, 1),)), dma((max(n_ctx - 1, 1),)),
            dma((1,)),
            dma((2,)),
        ],
        compiler_params=pltpu.CompilerParams(
            collective_id=0, has_side_effects=True, vmem_limit_bytes=40 * 1024 * 1024
        ),
    )(
        pltpu.with_memory_space_constraint(inputs, pltpu.HBM),
        pltpu.with_memory_space_constraint(upstream, pltpu.HBM),
        pltpu.with_memory_space_constraint(short_filter, pltpu.HBM),
        pltpu.with_memory_space_constraint(medium_filter.transpose(0, 2, 1), pltpu.HBM),
    )
    incoming, short_part, medium_part = pl.pallas_call(
        partial(place, tiles),
        out_shape=(
            jax.ShapeDtypeStruct(inputs.shape, BF16),
            jax.ShapeDtypeStruct(short_part.shape, F32),
            jax.ShapeDtypeStruct(medium_part.shape, F32),
        ),
        in_specs=[pl.BlockSpec(memory_space=pl.ANY)] * 3,
        out_specs=(hbm,) * 3,
        scratch_shapes=[dma((tiles + 2,))],
        compiler_params=pltpu.CompilerParams(vmem_limit_bytes=16 * 1024 * 1024),
    )(incoming, short_part, medium_part)
    return incoming, short_part.transpose(1, 0, 2), medium_part.transpose(0, 2, 1)


def solution(mesh):
    in_specs = (
        P("section", "ctx", "dp"),
        P("section", "ctx", "dp"),
        P("section", None, "dp"),
        P("section", None, "dp"),
    )
    out_specs = (
        P("section", "ctx", "dp"),
        P("section", None, ("dp", "ctx")),
        P("section", None, ("dp", "ctx")),
    )
    return jax.shard_map(
        partial(per_device, mesh.shape["ctx"], mesh.shape["section"]),
        mesh=mesh, in_specs=in_specs, out_specs=out_specs, check_vma=False,
    )
```

```python
from functools import partial

import jax
import jax.numpy as jnp
from jax import lax
from jax.experimental import pallas as pl
from jax.experimental.pallas import tpu as pltpu
from jax.sharding import PartitionSpec as P

MESH = pl.DeviceIdType.MESH
F32 = jnp.float32
BF16 = jnp.bfloat16
LANES = 128
RIM = 8
CHUNK = 64


def iota(shape, dim):
    return lax.broadcasted_iota(jnp.int32, shape, dim)


def kernel(
    dims,
    x_ref, gy_ref, sf_ref, mf_ref,
    out_ref, gs_ref, gm_ref,
    xv, gyv, hf, hb, wsc, tm, tk, xf, xrim, kvp, gext, keyb, valb, ef, ot, zb, grads_m, grads_s, snd, rcv, tr,
    bx_s, bx_r, kv_s, kv_r, ga_s, ga_r, er_s, er_r, ou_s, ou_r, gr_s, gr_r, z_sem, in_sem,
):
    n_ctx, n_sec, rows, tiles, lags, taps, width = dims
    c = lax.axis_index("ctx")
    s = lax.axis_index("section")
    nxt = lax.rem(c + 1, n_ctx)
    prv = lax.rem(c + n_ctx - 1, n_ctx)
    has_next = c < n_ctx - 1
    has_prev = c > 0
    sends_out = s > 0
    gets_out = s < n_sec - 1
    down = lax.rem(s + n_sec - 1, n_sec)
    up = lax.rem(s + 1, n_sec)
    gpt = LANES // width
    groups = gpt * tiles
    gpd = groups // n_ctx
    nb = rows // taps
    span = 2 * taps
    features = 3

    def load_x():
        return pltpu.make_async_copy(x_ref.at[0], xv, in_sem.at[0])

    def load_gy():
        return pltpu.make_async_copy(gy_ref.at[0], gyv, in_sem.at[1])

    load_x().start()
    load_gy().start()

    barrier = pltpu.get_barrier_semaphore()
    for d in range(1, n_ctx):
        pl.semaphore_signal(
            barrier, inc=1, device_id={"ctx": lax.rem(c + d, n_ctx)}, device_id_type=MESH
        )

    @pl.when(sends_out)
    def _():
        pl.semaphore_signal(barrier, inc=1, device_id={"section": down}, device_id_type=MESH)

    @pl.when(gets_out)
    def _():
        pl.semaphore_signal(barrier, inc=1, device_id={"section": up}, device_id_type=MESH)

    def remote(src, dst, send, recv, where):
        return pltpu.make_async_remote_copy(
            src_ref=src, dst_ref=dst, send_sem=send, recv_sem=recv,
            device_id=where, device_id_type=MESH,
        )

    def x_copy():
        return remote(
            x_ref.at[0, pl.ds(rows - 16, 16)], xrim, bx_s.at[0], bx_r.at[0], {"ctx": nxt}
        )

    def kv_copy(k):
        return remote(
            kvp.at[k, pl.ds(rows, taps)], kvp.at[k, pl.ds(0, taps)],
            kv_s.at[k], kv_r.at[k], {"ctx": nxt},
        )

    def gate_copy(k):
        return remote(
            gext.at[k, pl.ds(0, taps)], gext.at[k, pl.ds(rows, taps)],
            ga_s.at[k], ga_r.at[k], {"ctx": prv},
        )

    def rim_copy(k):
        return remote(
            ef.at[k, :, pl.ds(0, RIM)], ef.at[k, :, pl.ds(rows, RIM)],
            er_s.at[k], er_r.at[k], {"ctx": prv},
        )

    def out_copy(k):
        return remote(
            ot.at[k], out_ref.at[k],
            ou_s.at[k], ou_r.at[k], {"section": down},
        )

    taps_in = mf_ref[0]
    dot_nt = partial(
        lax.dot_general, dimension_numbers=(((1,), (1,)), ((), ())), preferred_element_type=F32
    )
    row_j, col_m = iota((taps, span), 0), iota((taps, span), 1)
    flipped = jnp.dot(
        taps_in, (col_m == taps - row_j).astype(BF16), preferred_element_type=F32
    )
    straight = jnp.dot(taps_in, (col_m == row_j).astype(BF16), preferred_element_type=F32)
    spread = (iota((groups, tiles * LANES), 1) // width == iota((groups, tiles * LANES), 0))
    wide = jnp.dot(sf_ref[0], spread.astype(BF16), preferred_element_type=F32)
    for k in range(tiles):
        hf[k] = flipped[k * gpt : (k + 1) * gpt]
        hb[k] = straight[k * gpt : (k + 1) * gpt]
        wsc[k, 0 : features * lags] = wide[:, k * LANES : (k + 1) * LANES]

    def build(k, carry):
        for u in range(gpt):
            for rows_of, dest in ((hf, tm), (hb, tk)):
                line = jnp.broadcast_to(rows_of[k, u : u + 1], (taps, span))
                band = pltpu.roll(line, 0, 1, stride=1, stride_axis=0)
                dest[k, :, u * span : (u + 1) * span] = band.astype(BF16)
        return carry

    lax.fori_loop(0, tiles // 2, build, 0)

    pl.semaphore_wait(
        barrier, n_ctx - 1 + sends_out.astype(jnp.int32) + gets_out.astype(jnp.int32)
    )

    @pl.when(has_next)
    def _():
        x_copy().start()

    @pl.when(jnp.logical_not(has_prev))
    def _():
        xrim[...] = jnp.zeros_like(xrim)
        kvp[:, 0:taps] = jnp.zeros((tiles, taps, LANES), BF16)

    @pl.when(jnp.logical_not(has_next))
    def _():
        gext[:, rows : rows + taps] = jnp.zeros((tiles, taps, LANES), BF16)
        ef[:, :, rows : rows + RIM] = jnp.zeros((tiles, features, RIM, LANES), F32)

    def zero_copy():
        return pltpu.make_async_copy(zb, out_ref, z_sem.at[0])

    @pl.when(jnp.logical_not(gets_out))
    def _():
        zb[...] = jnp.zeros_like(zb)
        zero_copy().start()

    lax.fori_loop(tiles // 2, tiles, build, 0)

    @pl.when(has_prev)
    def _():
        x_copy().wait_recv()

    load_x().wait()
    load_gy().wait()

    def lane_slice(k):
        return pl.ds(pl.multiple_of(k * LANES, LANES), LANES)

    def feature_tile(k):
        xf[k, RIM : RIM + rows] = xv[:, lane_slice(k)].astype(F32)
        xf[k, 0:RIM] = xrim[:, lane_slice(k)].astype(F32)[16 - RIM :]
        for start in range(0, rows, CHUNK):
            sums = [jnp.zeros((CHUNK, LANES), F32) for _ in range(features)]
            for i in range(lags):
                window = xf[k, RIM + start - i : RIM + start - i + CHUNK]
                for f in range(features):
                    sums[f] = sums[f] + wsc[k, f * lags + i : f * lags + i + 1] * window
            q, key, val = [v.astype(BF16) for v in sums]
            here = slice(start, start + CHUNK)
            keyb[k, here] = key
            valb[k, here] = val
            kvp[k, taps + start : taps + start + CHUNK] = (
                key.astype(F32) * val.astype(F32)
            ).astype(BF16)
            gext[k, here] = (
                gyv[here, lane_slice(k)].astype(F32) * q.astype(F32)
            ).astype(BF16)

    def feature_sent(k):
        @pl.when(has_next)
        def _():
            kv_copy(k).start()

        @pl.when(has_prev)
        def _():
            gate_copy(k).start()

    lane_group = lax.rem(iota((1, nb * LANES), 1), LANES) // width
    masks = [(lane_group == u).astype(BF16) for u in range(gpt)]
    reverse = (iota((taps, taps), 0) + iota((taps, taps), 1) == taps - 1).astype(BF16)

    def windows(ref, k):
        return jnp.concatenate(
            [ref[k, b * taps : b * taps + span] for b in range(nb)], axis=1
        )

    def medium_ready(k):
        @pl.when(has_prev)
        def _():
            kv_copy(k).wait_recv()

        @pl.when(has_next)
        def _():
            gate_copy(k).wait_recv()

    def medium_sent(k):
        @pl.when(has_prev)
        def _():
            rim_copy(k).start()

    def medium_tile(k):
        kv_win = windows(kvp, k)
        gate_win = windows(gext, k)
        kv_all = jnp.concatenate([kv_win * m for m in masks], axis=0)
        mixed = jnp.dot(tm[k], kv_all, preferred_element_type=F32)
        gate_all = jnp.concatenate([gate_win * m for m in masks], axis=0)
        back = jnp.dot(tk[k], gate_all, preferred_element_type=F32)
        for b in range(nb):
            here = slice(b * taps, (b + 1) * taps)
            mix_b = mixed[:, b * LANES : (b + 1) * LANES]
            back_b = back[:, b * LANES : (b + 1) * LANES]
            ef[k, 0, here] = (
                gyv[here, lane_slice(k)].astype(F32) * mix_b
            ).astype(BF16).astype(F32)
            ef[k, 1, here] = (back_b * valb[k, here].astype(F32)).astype(BF16).astype(F32)
            ef[k, 2, here] = (back_b * keyb[k, here].astype(F32)).astype(BF16).astype(F32)

        kv_own = jnp.concatenate(
            [kvp[k, taps + b * taps : span + b * taps] for b in range(nb)], axis=1
        )
        kv_rev = jnp.dot(reverse, kv_own, preferred_element_type=F32).astype(BF16)
        lines = []
        crosses = dot_nt(jnp.concatenate([kv_rev * m for m in masks], axis=0), gate_win)
        for u in range(gpt):
            cross = crosses[u * taps : (u + 1) * taps]
            turned = pltpu.roll(cross, 0, 1, stride=1, stride_axis=0)
            lines.append(jnp.sum(turned, axis=0, keepdims=True))
        diag = pltpu.roll(jnp.concatenate(lines, axis=0), span - taps + 1, 1)
        grads_m[pl.ds(pl.multiple_of(k * gpt, gpt), gpt), :] = diag[:, 0:taps]

    gather = (iota((gpt, LANES), 1) // width == iota((gpt, LANES), 0)).astype(F32)

    def short_ready(k):
        @pl.when(has_next)
        def _():
            rim_copy(k).wait_recv()

    def short_sent(k):
        @pl.when(sends_out)
        def _():
            out_copy(k).start()

    def short_tile(k):
        sums = [jnp.zeros((8, LANES), F32) for _ in range(features * lags)]
        for start in range(0, rows, CHUNK):
            x_here = xf[k, RIM + start : RIM + start + CHUNK]
            total = jnp.zeros((CHUNK, LANES), F32)
            for f in range(features):
                for i in range(lags):
                    at = f * lags + i
                    e = ef[k, f, start + i : start + i + CHUNK]
                    total = total + wsc[k, at : at + 1] * e
                    sums[at] = sums[at] + jnp.sum(
                        (e * x_here).reshape(CHUNK // 8, 8, LANES), axis=0
                    )
            ot[k, start : start + CHUNK] = total.astype(BF16)

        flat = [jnp.sum(v, axis=0, keepdims=True) for v in sums]
        flat.append(jnp.zeros((LANES - features * lags, LANES), F32))
        flat = jnp.concatenate(flat, axis=0)
        grads_s[pl.ds(pl.multiple_of(k * gpt, gpt), gpt), :] = dot_nt(
            gather, flat, precision=lax.Precision.HIGHEST
        )

    def feature_step(k, carry):
        feature_tile(k)
        feature_sent(k)
        return carry

    lax.fori_loop(0, tiles, feature_step, 0)

    def medium_step(k, carry):
        medium_ready(k)
        medium_tile(k)
        medium_sent(k)
        return carry

    def short_step(k, carry):
        short_ready(k)
        short_tile(k)
        short_sent(k)
        return carry

    def both_step(k, carry):
        medium_ready(k)
        short_ready(k - lag)
        short_tile(k - lag)
        medium_tile(k)
        medium_sent(k)
        short_sent(k - lag)
        return carry

    lag = 4
    lax.fori_loop(0, lag, medium_step, 0)
    lax.fori_loop(lag, tiles, both_step, 0)
    lax.fori_loop(tiles - lag, tiles, short_step, 0)

    for p in range(n_ctx):
        snd[p, :, 0:taps] = grads_m[p * gpd : (p + 1) * gpd]
        snd[p, :, taps : taps + LANES] = grads_s[p * gpd : (p + 1) * gpd]

    def grad_copy(d):
        to = lax.rem(c + d, n_ctx)
        return remote(snd.at[to], rcv.at[d - 1], gr_s.at[d - 1], gr_r.at[d - 1], {"ctx": to})

    for d in range(1, n_ctx):
        grad_copy(d).start()
    total = snd[c]
    for d in range(1, n_ctx):
        grad_copy(d).wait_recv()
        total = total + rcv[d - 1]
    gm_ref[0] = total[:, 0:taps]
    tr[...] = jnp.zeros_like(tr)
    tr[0:gpd] = total[:, taps : taps + LANES]
    gs_ref[:, 0] = tr[...].T[0 : features * lags, 0:gpd]

    for d in range(1, n_ctx):
        grad_copy(d).wait_send()

    @pl.when(has_next)
    def _():
        x_copy().wait_send()

    def drain(k, carry):
        @pl.when(has_next)
        def _():
            kv_copy(k).wait_send()

        @pl.when(has_prev)
        def _():
            gate_copy(k).wait_send()
            rim_copy(k).wait_send()

        @pl.when(sends_out)
        def _():
            out_copy(k).wait_send()

        @pl.when(gets_out)
        def _():
            out_copy(k).wait_recv()

        return carry

    lax.fori_loop(0, tiles, drain, 0)

    @pl.when(jnp.logical_not(gets_out))
    def _():
        zero_copy().wait()


def place(tiles, tiled_ref, gs_in, gm_in, out_ref, gs_ref, gm_ref, sem):
    copies = [
        pltpu.make_async_copy(
            tiled_ref.at[k], out_ref.at[0, :, pl.ds(k * LANES, LANES)], sem.at[k]
        )
        for k in range(tiles)
    ]
    copies.append(pltpu.make_async_copy(gs_in, gs_ref, sem.at[tiles]))
    copies.append(pltpu.make_async_copy(gm_in, gm_ref, sem.at[tiles + 1]))
    for copy in copies:
        copy.start()
    for copy in copies:
        copy.wait()


def per_device(n_ctx, n_sec, inputs, upstream, short_filter, medium_filter):
    _, rows, chans = inputs.shape
    taps, groups = medium_filter.shape[1:]
    lags = short_filter.shape[1] // 3
    width = chans // groups
    tiles = chans // LANES
    gpt = LANES // width
    gpd = groups // n_ctx
    dims = (n_ctx, n_sec, rows, tiles, lags, taps, width)
    vmem = pl.BlockSpec(memory_space=pltpu.VMEM)
    dma = pltpu.SemaphoreType.DMA
    span = 2 * taps
    hbm = pl.BlockSpec(memory_space=pltpu.HBM)
    incoming, short_part, medium_part = pl.pallas_call(
        partial(kernel, dims),
        out_shape=(
            jax.ShapeDtypeStruct((tiles, rows, LANES), BF16),
            jax.ShapeDtypeStruct((3 * lags, 1, gpd), F32),
            jax.ShapeDtypeStruct((1, gpd, taps), F32),
        ),
        in_specs=[hbm, hbm, vmem, vmem],
        out_specs=(pl.BlockSpec(memory_space=pl.ANY), vmem, vmem),
        scratch_shapes=[
            pltpu.VMEM((rows, chans), BF16),
            pltpu.VMEM((rows, chans), BF16),
            pltpu.VMEM((tiles, gpt, span), F32),
            pltpu.VMEM((tiles, gpt, span), F32),
            pltpu.VMEM((tiles, 24, LANES), F32),
            pltpu.VMEM((tiles, taps, gpt * span), BF16),
            pltpu.VMEM((tiles, taps, gpt * span), BF16),
            pltpu.VMEM((tiles, rows + RIM, LANES), F32),
            pltpu.VMEM((16, chans), BF16),
            pltpu.VMEM((tiles, rows + taps, LANES), BF16),
            pltpu.VMEM((tiles, rows + taps, LANES), BF16),
            pltpu.VMEM((tiles, rows, LANES), BF16),
            pltpu.VMEM((tiles, rows, LANES), BF16),
            pltpu.VMEM((tiles, 3, rows + RIM, LANES), F32),
            pltpu.VMEM((tiles, rows, LANES), BF16),
            pltpu.VMEM((tiles, rows, LANES), BF16),
            pltpu.VMEM((groups, taps), F32),
            pltpu.VMEM((groups, LANES), F32),
            pltpu.VMEM((n_ctx, gpd, taps + LANES), F32),
            pltpu.VMEM((max(n_ctx - 1, 1), gpd, taps + LANES), F32),
            pltpu.VMEM((LANES, LANES), F32),
            dma((1,)), dma((1,)),
            dma((tiles,)), dma((tiles,)),
            dma((tiles,)), dma((tiles,)),
            dma((tiles,)), dma((tiles,)),
            dma((tiles,)), dma((tiles,)),
            dma((max(n_ctx - 1, 1),)), dma((max(n_ctx - 1, 1),)),
            dma((1,)),
            dma((2,)),
        ],
        compiler_params=pltpu.CompilerParams(
            collective_id=0, has_side_effects=True, vmem_limit_bytes=40 * 1024 * 1024
        ),
    )(
        pltpu.with_memory_space_constraint(inputs, pltpu.HBM),
        pltpu.with_memory_space_constraint(upstream, pltpu.HBM),
        pltpu.with_memory_space_constraint(short_filter, pltpu.HBM),
        pltpu.with_memory_space_constraint(medium_filter.transpose(0, 2, 1), pltpu.HBM),
    )
    incoming, short_part, medium_part = pl.pallas_call(
        partial(place, tiles),
        out_shape=(
            jax.ShapeDtypeStruct(inputs.shape, BF16),
            jax.ShapeDtypeStruct(short_part.shape, F32),
            jax.ShapeDtypeStruct(medium_part.shape, F32),
        ),
        in_specs=[pl.BlockSpec(memory_space=pl.ANY)] * 3,
        out_specs=(hbm,) * 3,
        scratch_shapes=[dma((tiles + 2,))],
        compiler_params=pltpu.CompilerParams(vmem_limit_bytes=16 * 1024 * 1024),
    )(incoming, short_part, medium_part)
    return incoming, short_part.transpose(1, 0, 2), medium_part.transpose(0, 2, 1)


def solution(mesh):
    in_specs = (
        P("section", "ctx", "dp"),
        P("section", "ctx", "dp"),
        P("section", None, "dp"),
        P("section", None, "dp"),
    )
    out_specs = (
        P("section", "ctx", "dp"),
        P("section", None, ("dp", "ctx")),
        P("section", None, ("dp", "ctx")),
    )
    return jax.shard_map(
        partial(per_device, mesh.shape["ctx"], mesh.shape["section"]),
        mesh=mesh, in_specs=in_specs, out_specs=out_specs, check_vma=False,
    )
```
